32 devices in a mesh: groups: 2 (over y), chan: 4 (over z), space: 2 (over x), dp: 2 (over core).
Axes of the slice: x: 2, y: 2, z: 4, core: 2. Of those that a mesh axis runs over, the one named last changes fastest.
Arguments:
- inputs: bfloat16 [4, 4, 16, 16, 512], P(('groups', 'dp'), 'space', None, None, 'chan'), parts along dimension 0, may hold values from -6 to 6
- weights: bfloat16 [27, 512, 512], P(None, 'chan'), may hold values from -0.0625 to 0.0625
- bias: float32 [512], P('chan'), may hold values from -3 to 3
- upstream: bfloat16 [4, 4, 16, 16, 512], P(('groups', 'dp'), 'space', None, None, 'chan'), parts along dimension 0, may hold values from -6 to 6
Outputs:
- activated: bfloat16 [4, 4, 16, 16, 512], P(('groups', 'dp'), 'space', None, None, 'chan'), parts along dimension 0
- grad_inputs: bfloat16 [4, 4, 16, 16, 512], P(('groups', 'dp'), 'space', None, None, 'chan'), parts along dimension 0
- grad_weights: float32 [54, 512, 512], P('groups', 'chan', ('space', 'dp')), parts along dimension 0
The draws below stay inside these ranges and needn't reach their ends.
There are 2 independent parts, one for each index of `groups`. The reference program is written for one: setup_inputs(seed, part) draws one part's arguments, and reference() takes and returns one part's arrays. A program takes and returns all parts, laid end to end along the dimension named above; an argument that names none is the same for every part. Nothing has to cross between parts.
All inputs are finite; a program needn't handle non-finite values.
Results may differ from the reference program's by a relative error of at most 0.0049.
Values may be sent and summed in bfloat16 or wider, within the bound.
A program may use at most 64 MiB of HBM per device.

```python
import math
import jax
import jax.numpy as jnp
from jax import lax

CIN = 512
COUT = 512
NY = 16
NZ = 16
MB = 2
NX = 4
N_DP = 2


def with_spikes(array, own_key, source, target, blocks, factor):
    owner, partner = [(jnp.arange(array.shape[axis_at]) // (array.shape[axis_at] // blocks)).reshape([-1 if axis == axis_at else 1 for axis in range(array.ndim)]) for axis_at in (source, target)]
    chosen = jax.random.permutation(own_key, blocks)[partner]
    strong = (owner == chosen) | (owner == (partner + blocks // 2) % blocks)
    return jnp.where(strong, factor * array, array)


def block_scale(own_key, dims, cuts, smallest, top_value):
    factor_of = 1.0
    for position, parts in cuts:
        draws = jax.random.uniform(jax.random.fold_in(jax.random.fold_in(own_key, 6), position), (parts,), jnp.float32, smallest / len(cuts), top_value / len(cuts))
        factor_of = factor_of * jnp.repeat(jnp.exp(draws), dims[position] // parts).reshape((-1,) + (1,) * (len(dims) - 1 - position))
    return factor_of


def gaussian(stream_key, extent, width, most, split=(), dtype=jnp.bfloat16):
    loudness = block_scale(stream_key, extent, split, -0.22, 0.18) if split else 1.0
    array = jax.random.normal(stream_key, extent, jnp.float32) * width * loudness
    return jnp.minimum(jnp.maximum(array, -most), most).astype(dtype)


def gaussian_with(rng, shape, scale, bound, split, heavy, dtype=jnp.bfloat16):
    array = scale * jax.random.normal(rng, shape, jnp.float32)
    if split:
        array = array * block_scale(rng, shape, split, -0.22, 0.18)
    return jnp.clip(with_spikes(array, jax.random.fold_in(rng, 3), *heavy), -bound, bound).astype(dtype)


def setup_inputs(seed: int = 0, part: int = 0) -> dict:
    arg_keys = jax.random.split(jax.random.key(seed), 5)
    part_splits = jax.random.split(jax.random.fold_in(arg_keys[4], part), 5)
    return {
        "inputs": gaussian(part_splits[0], (MB, NX, NY, NZ, CIN), 1.0, 6.0, ((0, 2), (1, 2), (4, 4))),
        "weights": gaussian_with(arg_keys[1], (27, CIN, COUT), (27 * CIN) ** -0.5, 0.0625, ((1, 4),), (1, 2, 4, 2.0)),
        "bias": gaussian(arg_keys[2], (COUT,), 0.5, 3.0, ((0, 4),), jnp.float32),
        "upstream": gaussian_with(part_splits[3], (MB, NX, NY, NZ, COUT), 1.0, 6.0, ((0, 2), (1, 2), (4, 4)), (1, 4, 4, 2.0)),
    }


tap_offsets = [(a, b, c) for a in (-1, 0, 1) for b in (-1, 0, 1) for c in (-1, 0, 1)]

def border(volume):
    return jnp.pad(volume, ((0, 0), (1, 1), (1, 1), (1, 1), (0, 0)))

def shifted(volume, a, b, c, direction):
    return volume[:, 1 + direction * a:1 + direction * a + NX, 1 + direction * b:1 + direction * b + NY, 1 + direction * c:1 + direction * c + NZ, :]

def reference(inputs, weights, bias, upstream):
    voxels = N_DP * NX * NY * NZ
    bordered = border(inputs)
    summed = jnp.zeros((voxels, COUT), jnp.float32)
    for k, (a, b, c) in enumerate(tap_offsets):
        tap_cols = shifted(bordered, a, b, c, 1).reshape(voxels, CIN)
        summed = summed + jnp.dot(tap_cols, weights[k], preferred_element_type=jnp.float32)
    preact = summed + bias[None, :]
    gate_value = jax.nn.sigmoid(preact)
    activated = (preact * gate_value).astype(jnp.bfloat16).reshape(N_DP, NX, NY, NZ, COUT)
    grad_pre = (upstream.reshape(voxels, COUT).astype(jnp.float32) * gate_value * (1.0 + preact * (1.0 - gate_value))).astype(jnp.bfloat16)
    framed = border(grad_pre.reshape(N_DP, NX, NY, NZ, COUT))
    grad_in = jnp.zeros((voxels, CIN), jnp.float32)
    grad_list = []
    for k, (a, b, c) in enumerate(tap_offsets):
        back_cols = shifted(framed, a, b, c, -1).reshape(voxels, COUT)
        grad_in = grad_in + lax.dot_general(back_cols, weights[k], (((1,), (1,)), ((), ())), preferred_element_type=jnp.float32)
        tap_cols = shifted(bordered, a, b, c, 1).reshape(voxels, CIN)
        grad_list.append(lax.dot_general(tap_cols, grad_pre, (((0,), (0,)), ((), ())), preferred_element_type=jnp.float32))
    grad_weights = jnp.stack(grad_list) * (1.0 / math.sqrt(voxels))
    grad_inputs = grad_in.astype(jnp.bfloat16).reshape(N_DP, NX, NY, NZ, CIN)
    return (activated, grad_inputs, grad_weights)
```

```python
import functools
import math

import jax
import jax.numpy as jnp
from jax import lax
from jax.experimental import pallas as pl
from jax.experimental.pallas import tpu as pltpu
from jax.sharding import PartitionSpec as P

tap_offsets = [(a, b, c) for a in (-1, 0, 1) for b in (-1, 0, 1) for c in (-1, 0, 1)]


def extended(array, sides, width):
    for axis, dim in sides:
        size, length = (lax.axis_size(axis), array.shape[dim])
        up = [(i, (i + 1) % size) for i in range(size - 1)]
        down = [(j, i) for i, j in up]
        last = lax.slice_in_dim(array, length - width, length, axis=dim)
        leading = lax.slice_in_dim(array, 0, width, axis=dim)
        before = lax.ppermute(last, axis, up)
        after = lax.ppermute(leading, axis, down)
        array = jnp.concatenate([before, array, after], axis=dim)
    return array


def spatial_pad(volume):
    return jnp.pad(volume, ((0, 0), (0, 0), (1, 1), (1, 1), (0, 0)))


def tap_slice(volume, a, b, c, width_x, width_y, width_z):
    return volume[:, 1 + a : 1 + a + width_x, 1 + b : 1 + b + width_y, 1 + c : 1 + c + width_z]


def local_plain(inputs, weights, bias, upstream):
    batch_size, width_x, width_y, width_z, group_width = inputs.shape
    voxels = batch_size * width_x * width_y * width_z
    tap_count = weights.shape[0]
    outputs_all = weights.shape[2]
    bordered = spatial_pad(extended(inputs, (("space", 1),), 1))
    stacked = jnp.concatenate(
        [
            tap_slice(bordered, a, b, c, width_x, width_y, width_z).reshape(voxels, group_width)
            for a, b, c in tap_offsets
        ],
        axis=1,
    )
    flat_weights = weights.reshape(tap_count * group_width, outputs_all)
    out_share = outputs_all // lax.axis_size("chan")
    summed = lax.psum_scatter(
        lax.dot_general(
            flat_weights, stacked, (((0,), (1,)), ((), ())), preferred_element_type=jnp.float32
        ),
        "chan",
        scatter_dimension=0,
        tiled=True,
    ).T
    preact = summed + bias[None, :]
    gate_value = jax.nn.sigmoid(preact)
    activated = (
        (preact * gate_value)
        .astype(jnp.bfloat16)
        .reshape(batch_size, width_x, width_y, width_z, out_share)
    )
    grad_flat = (
        upstream.reshape(voxels, out_share).astype(jnp.float32)
        * gate_value
        * (1.0 + preact * (1.0 - gate_value))
    )
    grad_pre = grad_flat.astype(jnp.bfloat16).reshape(
        batch_size, width_x, width_y, width_z, out_share
    )
    grad_full = lax.all_gather(grad_pre, "chan", axis=4, tiled=True)
    framed = extended(grad_full, (("space", 1),), 1)
    interior = framed[:, 1:-1].reshape(voxels, outputs_all)
    framed_all = spatial_pad(framed)
    padded_shape = framed_all.shape
    projected = lax.dot_general(
        framed_all.reshape(-1, outputs_all),
        flat_weights,
        (((1,), (1,)), ((), ())),
        preferred_element_type=jnp.float32,
    )
    projected = projected.reshape(
        padded_shape[0], padded_shape[1], padded_shape[2], padded_shape[3], tap_count, group_width
    )
    grad_in = jnp.zeros((batch_size, width_x, width_y, width_z, group_width), jnp.float32)
    for k, (a, b, c) in enumerate(tap_offsets):
        grad_in = (
            grad_in
            + projected[
                :, 1 - a : 1 - a + width_x, 1 - b : 1 - b + width_y, 1 - c : 1 - c + width_z, k, :
            ]
        )
    grad_inputs = grad_in.astype(jnp.bfloat16)
    weight_partial = lax.dot_general(
        stacked, interior, (((0,), (0,)), ((), ())), preferred_element_type=jnp.float32
    )
    weight_partial = weight_partial.reshape(tap_count, group_width, outputs_all)
    reduced = lax.psum_scatter(weight_partial, ("space", "dp"), scatter_dimension=2, tiled=True)
    total_voxels = voxels * lax.axis_size("space") * lax.axis_size("dp")
    grad_weights = reduced * (1.0 / math.sqrt(total_voxels))
    return (activated, grad_inputs, grad_weights)


MESH = pl.DeviceIdType.MESH
LANES = 128


def z_shifted(plane):
    width_y, width_z, lanes = plane.shape
    rows = width_y * width_z
    flat = plane.reshape(rows, lanes)
    wide = flat.astype(jnp.float32)
    z = lax.broadcasted_iota(jnp.int32, (rows, lanes), 0) % width_z
    low = jnp.where(z == 0, 0.0, pltpu.roll(wide, 1, 0)).astype(flat.dtype)
    high = jnp.where(z == width_z - 1, 0.0, pltpu.roll(wide, rows - 1, 0)).astype(flat.dtype)
    return jnp.concatenate([low, flat, high], axis=1)


def z_combined(triple, width_z):
    rows = triple.shape[0]
    z = lax.broadcasted_iota(jnp.int32, (rows, LANES), 0) % width_z
    from_low = pltpu.roll(triple[:, :LANES], rows - 1, 0)
    from_high = pltpu.roll(triple[:, 2 * LANES :], 1, 0)
    return (
        triple[:, LANES : 2 * LANES]
        + jnp.where(z == width_z - 1, 0.0, from_low)
        + jnp.where(z == 0, 0.0, from_high)
    )


def fused_kernel(
    chans, scale,
    x_ref, w_hbm, b_ref, u_ref,
    act_ref, gi_ref, gw_ref,
    w, xa, x3, h3, xt, acc, pb, rb, gpf, gpq, gi32, hs, hr,
    w_sem, xa_send, xa_recv, rs_send, rs_recv, ag_send, ag_recv, gq_send, gq_recv, hb_send, hb_recv,
):
    g, c = lax.axis_index("groups"), lax.axis_index("chan")
    s, d = lax.axis_index("space"), lax.axis_index("dp")
    o = 1 - s
    mine = 2 * s + d
    width_y, width_z = x_ref.shape[1], x_ref.shape[2]
    area = width_y * width_z
    order = (s, o)

    def partner(j):
        return (o if j >= 2 else s), ((1 - d) if j % 2 else d)

    def far(r):
        return lax.rem(c + r, chans), lax.rem(c + chans - r, chans)

    weight_copy = pltpu.make_async_copy(w_hbm, w, w_sem)
    weight_copy.start()
    barrier = pltpu.get_barrier_semaphore()
    for j in (1, 2, 3):
        ps, pd = partner(j)
        pl.semaphore_signal(barrier, inc=1, device_id=(g, c, ps, pd), device_id_type=MESH)
    for r in range(1, chans):
        pl.semaphore_signal(barrier, inc=1, device_id=(g, far(r)[0], s, d), device_id_type=MESH)
    pl.semaphore_wait(barrier, 3 + chans - 1)

    def x_copy(index, j, plane):
        ps, pd = partner(j)
        return pltpu.make_async_remote_copy(
            src_ref=x_ref.at[plane], dst_ref=xa.at[d, 2 * s + plane],
            send_sem=xa_send.at[index], recv_sem=xa_recv.at[index],
            device_id=(g, c, ps, pd), device_id_type=MESH)

    x_list = [(0, 2, o), (1, 2, s), (2, 1, 0), (3, 1, 1), (4, 3, 0), (5, 3, 1)]
    x_copies = [x_copy(*item) for item in x_list]
    for copy in x_copies:
        copy.start()

    def x_arrived(index, j, plane):
        ps, pd = partner(j)
        there = {0: s, 1: o}.get(index, plane)
        pltpu.make_async_remote_copy(
            src_ref=x_ref.at[there], dst_ref=xa.at[pd, 2 * ps + there],
            send_sem=xa_send.at[index], recv_sem=xa_recv.at[index],
            device_id=(g, c, ps, pd), device_id_type=MESH).wait_recv()
        return pd, 2 * ps + there

    for ref in (x3, gpf):
        lead = ref.shape[0] * ref.shape[1] if len(ref.shape) == 5 else ref.shape[0]
        blank = jnp.zeros((width_z, ref.shape[-1]), ref.dtype)
        for i in range(lead):
            at = (i // ref.shape[1], i % ref.shape[1]) if len(ref.shape) == 5 else (i,)
            ref[at + (0,)] = blank
            ref[at + (width_y + 1,)] = blank
    h3[0] = jnp.zeros(h3.shape[1:], h3.dtype)
    h3[width_y + 1] = jnp.zeros(h3.shape[1:], h3.dtype)
    planes = gpq.shape[1] - 2
    for crop in range(gpq.shape[0]):
        for edge in (0, planes + 1):
            gpq[crop, edge] = jnp.zeros(gpq.shape[2:], gpq.dtype)
        for plane in range(planes):
            gpq[crop, plane + 1, 0] = jnp.zeros(gpq.shape[3:], gpq.dtype)
            gpq[crop, plane + 1, width_y + 1] = jnp.zeros(gpq.shape[3:], gpq.dtype)

    def keep_columns(crop, plane, triple):
        xt[crop * planes + plane] = triple.T

    triples = []
    for p in (0, 1):
        triple = z_shifted(x_ref[p])
        x3[p, pl.ds(1, width_y)] = triple.reshape(width_y, width_z, 3 * LANES)
        triples.append(triple)

    def taps_of(a, b):
        return pl.ds(9 * (a + 1) + 3 * (b + 1), 3)

    def rows_of(ref, b):
        return ref[pl.ds(1 + b, width_y)].reshape(area, -1)

    def partial_out(sources):
        left = jnp.concatenate([rows_of(ref, b) for ref, a in sources for b in (-1, 0, 1)], axis=1)
        right = jnp.concatenate(
            [w[taps_of(a, b)].reshape(3 * LANES, -1) for ref, a in sources for b in (-1, 0, 1)], axis=0)
        return jnp.dot(left, right, preferred_element_type=jnp.float32)

    def rs_copy(r, ph):
        return pltpu.make_async_remote_copy(
            src_ref=pb.at[ph, far(r)[0]], dst_ref=rb.at[ph, r - 1],
            send_sem=rs_send.at[r - 1, ph], recv_sem=rs_recv.at[r - 1, ph],
            device_id=(g, far(r)[0], s, d), device_id_type=MESH)

    def forward(ph, sources):
        total = partial_out(sources)
        for t in range(chans):
            part = total[:, t * LANES : (t + 1) * LANES]
            acc[ph, t] = part
            pb[ph, t] = part.astype(pb.dtype)
        for r in range(1, chans):
            rs_copy(r, ph).start()

    weight_copy.wait()
    lean = 1 - 2 * s
    forward(0, [(x3.at[s], 0), (x3.at[o], lean)])
    at = x_arrived(*x_list[0])
    halo = z_shifted(xa[at])
    h3[pl.ds(1, width_y)] = halo.reshape(width_y, width_z, 3 * LANES)
    forward(1, [(x3.at[o], 0), (x3.at[s], -lean), (h3, lean)])
    keep_columns(*at, halo)
    for p in (0, 1):
        keep_columns(d, 2 * s + p, triples[p])
    for item in x_list[1:]:
        at = x_arrived(*item)
        keep_columns(*at, z_shifted(xa[at]))

    def ag_copy(r, ph):
        block = gpf.at[c, order[ph], pl.ds(1, width_y)]
        return pltpu.make_async_remote_copy(
            src_ref=block, dst_ref=block,
            send_sem=ag_send.at[r - 1, ph], recv_sem=ag_recv.at[r - 1, ph],
            device_id=(g, far(r)[0], s, d), device_id_type=MESH)

    def ag_arrived(r, ph):
        block = gpf.at[far(r)[1], order[ph], pl.ds(1, width_y)]
        pltpu.make_async_remote_copy(
            src_ref=block, dst_ref=block,
            send_sem=ag_send.at[r - 1, ph], recv_sem=ag_recv.at[r - 1, ph],
            device_id=(g, far(r)[0], s, d), device_id_type=MESH).wait_recv()

    for ph in (0, 1):
        plane = order[ph]
        preact = acc[ph, c] + b_ref[...]
        for r in range(1, chans):
            rs_copy(r, ph).wait_recv()
            preact = preact + rb[ph, r - 1].astype(jnp.float32)
        gate = jax.nn.sigmoid(preact)
        act_ref[plane] = (preact * gate).astype(act_ref.dtype).reshape(width_y, width_z, LANES)
        up = u_ref[plane].reshape(area, LANES).astype(jnp.float32)
        grad = up * gate * (1.0 + preact * (1.0 - gate))
        gpf[c, plane, pl.ds(1, width_y)] = grad.astype(gpf.dtype).reshape(width_y, width_z, LANES)
        for r in range(1, chans):
            ag_copy(r, ph).start()

    def gq_copy(t, j, ph, crop, where):
        return pltpu.make_async_remote_copy(
            src_ref=gpf.at[t, order[ph], pl.ds(1, width_y)],
            dst_ref=gpq.at[crop, where, pl.ds(1, width_y)],
            send_sem=gq_send.at[j - 1, ph], recv_sem=gq_recv.at[j - 1, ph],
            device_id=(g, c, t // 2, t % 2), device_id_type=MESH)

    for ph in (0, 1):
        here = 1 + 2 * s + order[ph]
        for r in range(chans):
            t = far(r)[1]
            if r:
                ag_arrived(r, ph)
            j = 2 * lax.rem(t // 2 + s, 2) + lax.rem(t % 2 + d, 2)

            @pl.when(t != mine)
            def _(t=t, j=j, ph=ph, here=here):
                gq_copy(t, j, ph, d, here).start()

            @pl.when(t == mine)
            def _(t=t, ph=ph, here=here):
                gpq[d, here, pl.ds(1, width_y)] = gpf[t, order[ph], pl.ds(1, width_y)]

    def back(sources):
        left = jnp.concatenate(
            [gpf[t, plane, pl.ds(1 - b, width_y)].reshape(area, LANES)
             for plane, a in sources for b in (-1, 0, 1) for t in range(chans)], axis=1)
        right = jnp.concatenate(
            [w[taps_of(a, b)].reshape(3 * LANES, -1) for plane, a in sources for b in (-1, 0, 1)], axis=1)
        triple = lax.dot_general(
            left, right, (((1,), (1,)), ((), ())), preferred_element_type=jnp.float32)
        return z_combined(triple, width_z)

    hs[...] = back([(o, lean)]).astype(hs.dtype)
    edge = pltpu.make_async_remote_copy(
        src_ref=hs, dst_ref=hr, send_sem=hb_send, recv_sem=hb_recv,
        device_id=(g, c, o, d), device_id_type=MESH)
    edge.start()
    gi_ref[s] = back([(s, 0), (o, -lean)]).astype(gi_ref.dtype).reshape(width_y, width_z, LANES)
    gi32[...] = back([(o, 0), (s, lean)])

    for ph in (0, 1):
        for j in (1, 2, 3):
            ps, pd = partner(j)
            there = ps if ph == 0 else 1 - ps
            gq_copy(2 * ps + pd, j, ph, pd, 1 + 2 * ps + there).wait_recv()

    def weight_step(step, carry):
        a, b = step // 3 - 1, step % 3 - 1
        left = jnp.concatenate([xt[i] for i in range(xt.shape[0])], axis=1)
        right = gpq[:, pl.ds(1 - a, planes), pl.ds(1 - b, width_y)].reshape(-1, LANES)
        product = jnp.dot(left, right, preferred_element_type=jnp.float32)
        gw_ref[pl.ds(3 * step, 3)] = (product * scale).reshape(3, LANES, LANES)
        return carry

    lax.fori_loop(0, 9, weight_step, 0)

    edge.wait_recv()
    gi_ref[o] = (gi32[...] + hr[...].astype(jnp.float32)).astype(gi_ref.dtype).reshape(
        width_y, width_z, LANES)

    edge.wait_send()
    for copy in x_copies:
        copy.wait_send()
    for ph in (0, 1):
        for r in range(1, chans):
            rs_copy(r, ph).wait_send()
            ag_copy(r, ph).wait_send()
        for j in (1, 2, 3):
            ps, pd = partner(j)
            gq_copy(2 * ps + pd, j, ph, d, 1 + 2 * s + order[ph]).wait_send()


def local_fused(inputs, weights, bias, upstream):
    _, width_x, width_y, width_z, lanes = inputs.shape
    tap_count, _, outputs_all = weights.shape
    chans, crops = lax.axis_size("chan"), lax.axis_size("dp")
    planes = width_x * lax.axis_size("space")
    area = width_y * width_z
    half, full = jnp.bfloat16, jnp.float32
    slab = (width_x, width_y, width_z, lanes)
    dma = pltpu.SemaphoreType.DMA
    vmem = pl.BlockSpec(memory_space=pltpu.VMEM)
    flops = 3 * 2 * width_x * area * tap_count * lanes * outputs_all
    activated, grad_inputs, grad_weights = pl.pallas_call(
        functools.partial(fused_kernel, chans, 1.0 / math.sqrt(crops * planes * area)),
        out_shape=[
            jax.ShapeDtypeStruct(slab, half),
            jax.ShapeDtypeStruct(slab, half),
            jax.ShapeDtypeStruct((tap_count, lanes, lanes), full),
        ],
        in_specs=[vmem, pl.BlockSpec(memory_space=pl.ANY), vmem, vmem],
        out_specs=[vmem] * 3,
        scratch_shapes=[
            pltpu.VMEM(weights.shape, half),
            pltpu.VMEM((crops, planes, width_y, width_z, lanes), half),
            pltpu.VMEM((width_x, width_y + 2, width_z, 3 * lanes), half),
            pltpu.VMEM((width_y + 2, width_z, 3 * lanes), half),
            pltpu.VMEM((crops * planes, 3 * lanes, area), half),
            pltpu.VMEM((2, chans, area, lanes), full),
            pltpu.VMEM((2, chans, area, lanes), half),
            pltpu.VMEM((2, chans - 1, area, lanes), half),
            pltpu.VMEM((chans, width_x, width_y + 2, width_z, lanes), half),
            pltpu.VMEM((crops, planes + 2, width_y + 2, width_z, lanes), half),
            pltpu.VMEM((area, lanes), full),
            pltpu.VMEM((area, lanes), half),
            pltpu.VMEM((area, lanes), half),
            dma, dma((6,)), dma((6,)),
            dma((chans - 1, 2)), dma((chans - 1, 2)),
            dma((chans - 1, 2)), dma((chans - 1, 2)),
            dma((3, 2)), dma((3, 2)), dma, dma,
        ],
        compiler_params=pltpu.CompilerParams(
            collective_id=0, has_side_effects=True, vmem_limit_bytes=48 * 1024 * 1024),
        cost_estimate=pl.CostEstimate(
            flops=flops, bytes_accessed=2 * weights.size + 4 * tap_count * lanes * lanes,
            transcendentals=width_x * area * lanes),
    )(inputs.reshape(slab), weights, bias.reshape(1, lanes), upstream.reshape(slab))
    return activated[None], grad_inputs[None], grad_weights


def local(inputs, weights, bias, upstream):
    fits = (
        inputs.shape[0] == 1
        and inputs.shape[1] == 2
        and inputs.shape[3] % 16 == 0
        and inputs.shape[4] == upstream.shape[4] == LANES
        and weights.shape[2] == LANES * lax.axis_size("chan")
        and lax.axis_size("chan") == 4
        and lax.axis_size("space") == 2
        and lax.axis_size("dp") == 2
    )
    return (local_fused if fits else local_plain)(inputs, weights, bias, upstream)


def solution(mesh):
    return jax.shard_map(
        local,
        mesh=mesh,
        in_specs=(
            P(("groups", "dp"), "space", None, None, "chan"),
            P(None, "chan", None),
            P("chan"),
            P(("groups", "dp"), "space", None, None, "chan"),
        ),
        out_specs=(
            P(("groups", "dp"), "space", None, None, "chan"),
            P(("groups", "dp"), "space", None, None, "chan"),
            P("groups", "chan", ("space", "dp")),
        ),
        check_vma=False,
    )
```

```python
import functools
import math

import jax
import jax.numpy as jnp
from jax import lax
from jax.experimental import pallas as pl
from jax.experimental.pallas import tpu as pltpu
from jax.sharding import PartitionSpec as P

tap_offsets = [(a, b, c) for a in (-1, 0, 1) for b in (-1, 0, 1) for c in (-1, 0, 1)]


def extended(array, sides, width):
    for axis, dim in sides:
        size, length = (lax.axis_size(axis), array.shape[dim])
        up = [(i, (i + 1) % size) for i in range(size - 1)]
        down = [(j, i) for i, j in up]
        last = lax.slice_in_dim(array, length - width, length, axis=dim)
        leading = lax.slice_in_dim(array, 0, width, axis=dim)
        before = lax.ppermute(last, axis, up)
        after = lax.ppermute(leading, axis, down)
        array = jnp.concatenate([before, array, after], axis=dim)
    return array


def spatial_pad(volume):
    return jnp.pad(volume, ((0, 0), (0, 0), (1, 1), (1, 1), (0, 0)))


def tap_slice(volume, a, b, c, width_x, width_y, width_z):
    return volume[:, 1 + a : 1 + a + width_x, 1 + b : 1 + b + width_y, 1 + c : 1 + c + width_z]


def local_plain(inputs, weights, bias, upstream):
    batch_size, width_x, width_y, width_z, group_width = inputs.shape
    voxels = batch_size * width_x * width_y * width_z
    tap_count = weights.shape[0]
    outputs_all = weights.shape[2]
    bordered = spatial_pad(extended(inputs, (("space", 1),), 1))
    stacked = jnp.concatenate(
        [
            tap_slice(bordered, a, b, c, width_x, width_y, width_z).reshape(voxels, group_width)
            for a, b, c in tap_offsets
        ],
        axis=1,
    )
    flat_weights = weights.reshape(tap_count * group_width, outputs_all)
    out_share = outputs_all // lax.axis_size("chan")
    summed = lax.psum_scatter(
        lax.dot_general(
            flat_weights, stacked, (((0,), (1,)), ((), ())), preferred_element_type=jnp.float32
        ),
        "chan",
        scatter_dimension=0,
        tiled=True,
    ).T
    preact = summed + bias[None, :]
    gate_value = jax.nn.sigmoid(preact)
    activated = (
        (preact * gate_value)
        .astype(jnp.bfloat16)
        .reshape(batch_size, width_x, width_y, width_z, out_share)
    )
    grad_flat = (
        upstream.reshape(voxels, out_share).astype(jnp.float32)
        * gate_value
        * (1.0 + preact * (1.0 - gate_value))
    )
    grad_pre = grad_flat.astype(jnp.bfloat16).reshape(
        batch_size, width_x, width_y, width_z, out_share
    )
    grad_full = lax.all_gather(grad_pre, "chan", axis=4, tiled=True)
    framed = extended(grad_full, (("space", 1),), 1)
    interior = framed[:, 1:-1].reshape(voxels, outputs_all)
    framed_all = spatial_pad(framed)
    padded_shape = framed_all.shape
    projected = lax.dot_general(
        framed_all.reshape(-1, outputs_all),
        flat_weights,
        (((1,), (1,)), ((), ())),
        preferred_element_type=jnp.float32,
    )
    projected = projected.reshape(
        padded_shape[0], padded_shape[1], padded_shape[2], padded_shape[3], tap_count, group_width
    )
    grad_in = jnp.zeros((batch_size, width_x, width_y, width_z, group_width), jnp.float32)
    for k, (a, b, c) in enumerate(tap_offsets):
        grad_in = (
            grad_in
            + projected[
                :, 1 - a : 1 - a + width_x, 1 - b : 1 - b + width_y, 1 - c : 1 - c + width_z, k, :
            ]
        )
    grad_inputs = grad_in.astype(jnp.bfloat16)
    weight_partial = lax.dot_general(
        stacked, interior, (((0,), (0,)), ((), ())), preferred_element_type=jnp.float32
    )
    weight_partial = weight_partial.reshape(tap_count, group_width, outputs_all)
    reduced = lax.psum_scatter(weight_partial, ("space", "dp"), scatter_dimension=2, tiled=True)
    total_voxels = voxels * lax.axis_size("space") * lax.axis_size("dp")
    grad_weights = reduced * (1.0 / math.sqrt(total_voxels))
    return (activated, grad_inputs, grad_weights)


MESH = pl.DeviceIdType.MESH
LANES = 128


def z_shifted(plane):
    width_y, width_z, lanes = plane.shape
    rows = width_y * width_z
    flat = plane.reshape(rows, lanes)
    wide = flat.astype(jnp.float32)
    z = lax.broadcasted_iota(jnp.int32, (rows, lanes), 0) % width_z
    low = jnp.where(z == 0, 0.0, pltpu.roll(wide, 1, 0)).astype(flat.dtype)
    high = jnp.where(z == width_z - 1, 0.0, pltpu.roll(wide, rows - 1, 0)).astype(flat.dtype)
    return jnp.concatenate([low, flat, high], axis=1)


def z_combined(triple, width_z):
    rows = triple.shape[0]
    z = lax.broadcasted_iota(jnp.int32, (rows, LANES), 0) % width_z
    from_low = pltpu.roll(triple[:, :LANES], rows - 1, 0)
    from_high = pltpu.roll(triple[:, 2 * LANES :], 1, 0)
    return (
        triple[:, LANES : 2 * LANES]
        + jnp.where(z == width_z - 1, 0.0, from_low)
        + jnp.where(z == 0, 0.0, from_high)
    )


def fused_kernel(
    chans, scale,
    x_hbm, w_hbm, b_hbm, u_hbm,
    act_ref, gi_ref, gw_ref,
    x_ref, b_ref, u_ref, w, xa, x3, h3, xt, acc, pb, rb, gpf, gpq, gi32, hs, hr,
    in_sem, xa_send, xa_recv, rs_send, rs_recv, ag_send, ag_recv, gq_send, gq_recv, hb_send, hb_recv,
):
    g, c = lax.axis_index("groups"), lax.axis_index("chan")
    s, d = lax.axis_index("space"), lax.axis_index("dp")
    o = 1 - s
    mine = 2 * s + d
    width_y, width_z = x_ref.shape[1], x_ref.shape[2]
    area = width_y * width_z
    order = (s, o)

    def partner(j):
        return (o if j >= 2 else s), ((1 - d) if j % 2 else d)

    def far(r):
        return lax.rem(c + r, chans), lax.rem(c + chans - r, chans)

    loads = [
        pltpu.make_async_copy(source, target, in_sem.at[i])
        for i, (source, target) in enumerate(
            ((x_hbm, x_ref), (w_hbm, w), (b_hbm, b_ref), (u_hbm, u_ref)))
    ]
    for load in loads:
        load.start()
    barrier = pltpu.get_barrier_semaphore()
    for j in (1, 2, 3):
        ps, pd = partner(j)
        pl.semaphore_signal(barrier, inc=1, device_id=(g, c, ps, pd), device_id_type=MESH)
    for r in range(1, chans):
        pl.semaphore_signal(barrier, inc=1, device_id=(g, far(r)[0], s, d), device_id_type=MESH)

    def x_copy(index, j, plane):
        ps, pd = partner(j)
        return pltpu.make_async_remote_copy(
            src_ref=x_hbm.at[plane], dst_ref=xa.at[d, 2 * s + plane],
            send_sem=xa_send.at[index], recv_sem=xa_recv.at[index],
            device_id=(g, c, ps, pd), device_id_type=MESH)

    x_list = [(0, 2, o), (1, 2, s), (2, 1, 0), (3, 1, 1), (4, 3, 0), (5, 3, 1)]
    x_copies = [x_copy(*item) for item in x_list]

    def x_arrived(index, j, plane):
        ps, pd = partner(j)
        there = {0: s, 1: o}.get(index, plane)
        pltpu.make_async_remote_copy(
            src_ref=x_hbm.at[there], dst_ref=xa.at[pd, 2 * ps + there],
            send_sem=xa_send.at[index], recv_sem=xa_recv.at[index],
            device_id=(g, c, ps, pd), device_id_type=MESH).wait_recv()
        return pd, 2 * ps + there

    def blank_rows(ref, at):
        blank = jnp.zeros(ref.shape[-2:], ref.dtype)
        ref[at + (0,)] = blank
        ref[at + (width_y + 1,)] = blank

    for p in (0, 1):
        blank_rows(x3, (p,))

    def keep_columns(crop, plane, triple):
        xt[crop * gpq.shape[1] + plane] = triple.T

    loads[0].wait()
    triples = []
    for p in (0, 1):
        triple = z_shifted(x_ref[p])
        x3[p, pl.ds(1, width_y)] = triple.reshape(width_y, width_z, 3 * LANES)
        triples.append(triple)

    def taps_of(a, b):
        return pl.ds(9 * (a + 1) + 3 * (b + 1), 3)

    def rows_of(ref, b):
        return ref[pl.ds(1 + b, width_y)].reshape(area, -1)

    def partial_out(sources):
        left = jnp.concatenate([rows_of(ref, b) for ref, a in sources for b in (-1, 0, 1)], axis=1)
        right = jnp.concatenate(
            [w[taps_of(a, b)].reshape(3 * LANES, -1) for ref, a in sources for b in (-1, 0, 1)], axis=0)
        return jnp.dot(left, right, preferred_element_type=jnp.float32)

    def rs_copy(r, ph):
        return pltpu.make_async_remote_copy(
            src_ref=pb.at[ph, far(r)[0]], dst_ref=rb.at[ph, r - 1],
            send_sem=rs_send.at[r - 1, ph], recv_sem=rs_recv.at[r - 1, ph],
            device_id=(g, far(r)[0], s, d), device_id_type=MESH)

    def forward(ph, sources):
        total = partial_out(sources)
        for t in range(chans):
            part = total[:, t * LANES : (t + 1) * LANES]
            acc[ph, t] = part
            pb[ph, t] = part.astype(pb.dtype)

    def scatter(ph):
        for r in range(1, chans):
            rs_copy(r, ph).start()

    loads[1].wait()
    lean = 1 - 2 * s
    forward(0, [(x3.at[s], 0), (x3.at[o], lean)])
    pl.semaphore_wait(barrier, 3 + chans - 1)
    scatter(0)
    for copy in x_copies:
        copy.start()
    blank_rows(h3, ())
    for t in range(chans):
        for p in (0, 1):
            blank_rows(gpf, (t, p))
    planes = gpq.shape[1]
    for crop in range(gpq.shape[0]):
        for p in range(planes):
            blank_rows(gpq, (crop, p))
    at = x_arrived(*x_list[0])
    halo = z_shifted(xa[at])
    h3[pl.ds(1, width_y)] = halo.reshape(width_y, width_z, 3 * LANES)
    forward(1, [(x3.at[o], 0), (x3.at[s], -lean), (h3, lean)])
    scatter(1)
    keep_columns(*at, halo)
    for p in (0, 1):
        keep_columns(d, 2 * s + p, triples[p])
    for item in x_list[1:]:
        at = x_arrived(*item)
        keep_columns(*at, z_shifted(xa[at]))

    def ag_copy(r, ph):
        block = gpf.at[c, order[ph], pl.ds(1, width_y)]
        return pltpu.make_async_remote_copy(
            src_ref=block, dst_ref=block,
            send_sem=ag_send.at[r - 1, ph], recv_sem=ag_recv.at[r - 1, ph],
            device_id=(g, far(r)[0], s, d), device_id_type=MESH)

    def ag_arrived(r, ph):
        block = gpf.at[far(r)[1], order[ph], pl.ds(1, width_y)]
        pltpu.make_async_remote_copy(
            src_ref=block, dst_ref=block,
            send_sem=ag_send.at[r - 1, ph], recv_sem=ag_recv.at[r - 1, ph],
            device_id=(g, far(r)[0], s, d), device_id_type=MESH).wait_recv()

    loads[2].wait()
    loads[3].wait()
    for ph in (0, 1):
        plane = order[ph]
        preact = acc[ph, c] + b_ref[...]
        for r in range(1, chans):
            rs_copy(r, ph).wait_recv()
            preact = preact + rb[ph, r - 1].astype(jnp.float32)
        gate = jax.nn.sigmoid(preact)
        act_ref[plane] = (preact * gate).astype(act_ref.dtype).reshape(width_y, width_z, LANES)
        up = u_ref[plane].reshape(area, LANES).astype(jnp.float32)
        grad = up * gate * (1.0 + preact * (1.0 - gate))
        gpf[c, plane, pl.ds(1, width_y)] = grad.astype(gpf.dtype).reshape(width_y, width_z, LANES)
        for r in range(1, chans):
            ag_copy(r, ph).start()

    def gq_copy(t, j, ph, crop, where):
        return pltpu.make_async_remote_copy(
            src_ref=gpf.at[t, order[ph], pl.ds(1, width_y)],
            dst_ref=gpq.at[crop, where, pl.ds(1, width_y)],
            send_sem=gq_send.at[j - 1, ph], recv_sem=gq_recv.at[j - 1, ph],
            device_id=(g, c, t // 2, t % 2), device_id_type=MESH)

    def spread(ph):
        here = 2 * s + order[ph]
        for r in range(chans):
            t = far(r)[1]
            if r:
                ag_arrived(r, ph)
            j = 2 * lax.rem(t // 2 + s, 2) + lax.rem(t % 2 + d, 2)

            @pl.when(t != mine)
            def _(t=t, j=j):
                gq_copy(t, j, ph, d, here).start()

            @pl.when(t == mine)
            def _(t=t):
                gpq[d, here, pl.ds(1, width_y)] = gpf[t, order[ph], pl.ds(1, width_y)]

    def back(plane, a):
        left = jnp.concatenate(
            [gpf[t, plane, pl.ds(1 - b, width_y)].reshape(area, LANES)
             for b in (-1, 0, 1) for t in range(chans)], axis=1)
        right = jnp.concatenate(
            [w[taps_of(a, b)].reshape(3 * LANES, -1) for b in (-1, 0, 1)], axis=1)
        triple = lax.dot_general(
            left, right, (((1,), (1,)), ((), ())), preferred_element_type=jnp.float32)
        return z_combined(triple, width_z)

    def collected(ph):
        for j in (1, 2, 3):
            ps, pd = partner(j)
            there = ps if ph == 0 else 1 - ps
            gq_copy(2 * ps + pd, j, ph, pd, 2 * ps + there).wait_recv()

    def weight_part(ph):
        held = (0, 3) if ph == 0 else (1, 2)
        crops = range(gpq.shape[0])

        def step(i, carry):
            for a in (-1, 0, 1):
                pairs = [(crop, v) for crop in crops for v in held if 0 <= v + a < planes]
                left = jnp.concatenate([xt[crop * planes + v + a] for crop, v in pairs], axis=1)
                right = jnp.concatenate(
                    [gpq[crop, v, pl.ds(2 - i, width_y)].reshape(area, LANES) for crop, v in pairs],
                    axis=0)
                product = jnp.dot(left, right, preferred_element_type=jnp.float32)
                product = product.reshape(3, LANES, LANES)
                at = pl.ds(9 * (a + 1) + 3 * i, 3)
                gw_ref[at] = product if ph == 0 else (gw_ref[at] + product) * scale
            return carry

        lax.fori_loop(0, 3, step, 0)

    spread(0)
    gi32[0] = back(s, 0)
    gi32[1] = back(s, lean)
    collected(0)
    weight_part(0)
    spread(1)
    hs[...] = back(o, lean).astype(hs.dtype)
    edge = pltpu.make_async_remote_copy(
        src_ref=hs, dst_ref=hr, send_sem=hb_send, recv_sem=hb_recv,
        device_id=(g, c, o, d), device_id_type=MESH)
    edge.start()
    gi_ref[s] = (gi32[0] + back(o, -lean)).astype(gi_ref.dtype).reshape(width_y, width_z, LANES)
    gi32[1] = gi32[1] + back(o, 0)
    collected(1)
    weight_part(1)

    edge.wait_recv()
    gi_ref[o] = (gi32[1] + hr[...].astype(jnp.float32)).astype(gi_ref.dtype).reshape(
        width_y, width_z, LANES)

    edge.wait_send()
    for copy in x_copies:
        copy.wait_send()
    for ph in (0, 1):
        for r in range(1, chans):
            rs_copy(r, ph).wait_send()
            ag_copy(r, ph).wait_send()
        for j in (1, 2, 3):
            ps, pd = partner(j)
            gq_copy(2 * ps + pd, j, ph, d, 2 * s + order[ph]).wait_send()


def local_fused(inputs, weights, bias, upstream):
    _, width_x, width_y, width_z, lanes = inputs.shape
    tap_count, _, outputs_all = weights.shape
    chans, crops = lax.axis_size("chan"), lax.axis_size("dp")
    planes = width_x * lax.axis_size("space")
    area = width_y * width_z
    half, full = jnp.bfloat16, jnp.float32
    slab = (width_x, width_y, width_z, lanes)
    dma = pltpu.SemaphoreType.DMA
    vmem = pl.BlockSpec(memory_space=pltpu.VMEM)
    flops = 3 * 2 * width_x * area * tap_count * lanes * outputs_all
    activated, grad_inputs, grad_weights = pl.pallas_call(
        functools.partial(fused_kernel, chans, 1.0 / math.sqrt(crops * planes * area)),
        out_shape=[
            jax.ShapeDtypeStruct(slab, half),
            jax.ShapeDtypeStruct(slab, half),
            jax.ShapeDtypeStruct((tap_count, lanes, lanes), full),
        ],
        in_specs=[pl.BlockSpec(memory_space=pltpu.HBM)] * 4,
        out_specs=[vmem] * 3,
        scratch_shapes=[
            pltpu.VMEM(slab, half),
            pltpu.VMEM((1, lanes), full),
            pltpu.VMEM(slab, half),
            pltpu.VMEM(weights.shape, half),
            pltpu.VMEM((crops, planes, width_y, width_z, lanes), half),
            pltpu.VMEM((width_x, width_y + 2, width_z, 3 * lanes), half),
            pltpu.VMEM((width_y + 2, width_z, 3 * lanes), half),
            pltpu.VMEM((crops * planes, 3 * lanes, area), half),
            pltpu.VMEM((2, chans, area, lanes), full),
            pltpu.VMEM((2, chans, area, lanes), half),
            pltpu.VMEM((2, chans - 1, area, lanes), half),
            pltpu.VMEM((chans, width_x, width_y + 2, width_z, lanes), half),
            pltpu.VMEM((crops, planes, width_y + 2, width_z, lanes), half),
            pltpu.VMEM((2, area, lanes), full),
            pltpu.VMEM((area, lanes), half),
            pltpu.VMEM((area, lanes), half),
            dma((4,)), dma((6,)), dma((6,)),
            dma((chans - 1, 2)), dma((chans - 1, 2)),
            dma((chans - 1, 2)), dma((chans - 1, 2)),
            dma((3, 2)), dma((3, 2)), dma, dma,
        ],
        compiler_params=pltpu.CompilerParams(
            collective_id=0, has_side_effects=True, vmem_limit_bytes=60 * 1024 * 1024),
        cost_estimate=pl.CostEstimate(
            flops=flops, bytes_accessed=2 * weights.size + 4 * tap_count * lanes * lanes,
            transcendentals=width_x * area * lanes),
    )(inputs.reshape(slab), weights, bias.reshape(1, lanes), upstream.reshape(slab))
    return activated[None], grad_inputs[None], grad_weights


def local(inputs, weights, bias, upstream):
    fits = (
        inputs.shape[0] == 1
        and inputs.shape[1] == 2
        and inputs.shape[3] % 16 == 0
        and inputs.shape[4] == upstream.shape[4] == LANES
        and weights.shape[2] == LANES * lax.axis_size("chan")
        and lax.axis_size("chan") == 4
        and lax.axis_size("space") == 2
        and lax.axis_size("dp") == 2
    )
    return (local_fused if fits else local_plain)(inputs, weights, bias, upstream)


def solution(mesh):
    return jax.shard_map(
        local,
        mesh=mesh,
        in_specs=(
            P(("groups", "dp"), "space", None, None, "chan"),
            P(None, "chan", None),
            P("chan"),
            P(("groups", "dp"), "space", None, None, "chan"),
        ),
        out_specs=(
            P(("groups", "dp"), "space", None, None, "chan"),
            P(("groups", "dp"), "space", None, None, "chan"),
            P("groups", "chan", ("space", "dp")),
        ),
        check_vma=False,
    )
```

```python
import functools
import math

import jax
import jax.numpy as jnp
from jax import lax
from jax.experimental import pallas as pl
from jax.experimental.pallas import tpu as pltpu
from jax.sharding import PartitionSpec as P

tap_offsets = [(a, b, c) for a in (-1, 0, 1) for b in (-1, 0, 1) for c in (-1, 0, 1)]


def extended(array, sides, width):
    for axis, dim in sides:
        size, length = (lax.axis_size(axis), array.shape[dim])
        up = [(i, (i + 1) % size) for i in range(size - 1)]
        down = [(j, i) for i, j in up]
        last = lax.slice_in_dim(array, length - width, length, axis=dim)
        leading = lax.slice_in_dim(array, 0, width, axis=dim)
        before = lax.ppermute(last, axis, up)
        after = lax.ppermute(leading, axis, down)
        array = jnp.concatenate([before, array, after], axis=dim)
    return array


def spatial_pad(volume):
    return jnp.pad(volume, ((0, 0), (0, 0), (1, 1), (1, 1), (0, 0)))


def tap_slice(volume, a, b, c, width_x, width_y, width_z):
    return volume[:, 1 + a : 1 + a + width_x, 1 + b : 1 + b + width_y, 1 + c : 1 + c + width_z]


def local_plain(inputs, weights, bias, upstream):
    batch_size, width_x, width_y, width_z, group_width = inputs.shape
    voxels = batch_size * width_x * width_y * width_z
    tap_count = weights.shape[0]
    outputs_all = weights.shape[2]
    bordered = spatial_pad(extended(inputs, (("space", 1),), 1))
    stacked = jnp.concatenate(
        [
            tap_slice(bordered, a, b, c, width_x, width_y, width_z).reshape(voxels, group_width)
            for a, b, c in tap_offsets
        ],
        axis=1,
    )
    flat_weights = weights.reshape(tap_count * group_width, outputs_all)
    out_share = outputs_all // lax.axis_size("chan")
    summed = lax.psum_scatter(
        lax.dot_general(
            flat_weights, stacked, (((0,), (1,)), ((), ())), preferred_element_type=jnp.float32
        ),
        "chan",
        scatter_dimension=0,
        tiled=True,
    ).T
    preact = summed + bias[None, :]
    gate_value = jax.nn.sigmoid(preact)
    activated = (
        (preact * gate_value)
        .astype(jnp.bfloat16)
        .reshape(batch_size, width_x, width_y, width_z, out_share)
    )
    grad_flat = (
        upstream.reshape(voxels, out_share).astype(jnp.float32)
        * gate_value
        * (1.0 + preact * (1.0 - gate_value))
    )
    grad_pre = grad_flat.astype(jnp.bfloat16).reshape(
        batch_size, width_x, width_y, width_z, out_share
    )
    grad_full = lax.all_gather(grad_pre, "chan", axis=4, tiled=True)
    framed = extended(grad_full, (("space", 1),), 1)
    interior = framed[:, 1:-1].reshape(voxels, outputs_all)
    framed_all = spatial_pad(framed)
    padded_shape = framed_all.shape
    projected = lax.dot_general(
        framed_all.reshape(-1, outputs_all),
        flat_weights,
        (((1,), (1,)), ((), ())),
        preferred_element_type=jnp.float32,
    )
    projected = projected.reshape(
        padded_shape[0], padded_shape[1], padded_shape[2], padded_shape[3], tap_count, group_width
    )
    grad_in = jnp.zeros((batch_size, width_x, width_y, width_z, group_width), jnp.float32)
    for k, (a, b, c) in enumerate(tap_offsets):
        grad_in = (
            grad_in
            + projected[
                :, 1 - a : 1 - a + width_x, 1 - b : 1 - b + width_y, 1 - c : 1 - c + width_z, k, :
            ]
        )
    grad_inputs = grad_in.astype(jnp.bfloat16)
    weight_partial = lax.dot_general(
        stacked, interior, (((0,), (0,)), ((), ())), preferred_element_type=jnp.float32
    )
    weight_partial = weight_partial.reshape(tap_count, group_width, outputs_all)
    reduced = lax.psum_scatter(weight_partial, ("space", "dp"), scatter_dimension=2, tiled=True)
    total_voxels = voxels * lax.axis_size("space") * lax.axis_size("dp")
    grad_weights = reduced * (1.0 / math.sqrt(total_voxels))
    return (activated, grad_inputs, grad_weights)


MESH = pl.DeviceIdType.MESH
LANES = 128


def z_shifted(plane):
    width_y, width_z, lanes = plane.shape
    rows = width_y * width_z
    flat = plane.reshape(rows, lanes)
    wide = flat.astype(jnp.float32)
    z = lax.broadcasted_iota(jnp.int32, (rows, lanes), 0) % width_z
    low = jnp.where(z == 0, 0.0, pltpu.roll(wide, 1, 0)).astype(flat.dtype)
    high = jnp.where(z == width_z - 1, 0.0, pltpu.roll(wide, rows - 1, 0)).astype(flat.dtype)
    return jnp.concatenate([low, flat, high], axis=1)


def z_combined(triple, width_z):
    rows = triple.shape[0]
    z = lax.broadcasted_iota(jnp.int32, (rows, LANES), 0) % width_z
    from_low = pltpu.roll(triple[:, :LANES], rows - 1, 0)
    from_high = pltpu.roll(triple[:, 2 * LANES :], 1, 0)
    return (
        triple[:, LANES : 2 * LANES]
        + jnp.where(z == width_z - 1, 0.0, from_low)
        + jnp.where(z == 0, 0.0, from_high)
    )


def fused_kernel(
    chans,
    x_hbm, w_hbm, b_hbm, u_hbm,
    act_ref, gi_ref, gw_ref,
    x_ref, b_ref, u_ref, w, xa, x3, h3, xt, acc, pb, rb, gpf, gpq, gi32, hs, hr,
    in_sem, xa_send, xa_recv, rs_send, rs_recv, ag_send, ag_recv, gq_send, gq_recv, hb_send, hb_recv,
):
    g, c = lax.axis_index("groups"), lax.axis_index("chan")
    s, d = lax.axis_index("space"), lax.axis_index("dp")
    o = 1 - s
    mine = 2 * s + d
    width_y, width_z = x_ref.shape[1], x_ref.shape[2]
    area = width_y * width_z
    order = (s, o)

    def partner(j):
        return (o if j >= 2 else s), ((1 - d) if j % 2 else d)

    def far(r):
        return lax.rem(c + r, chans), lax.rem(c + chans - r, chans)

    loads = [
        pltpu.make_async_copy(source, target, in_sem.at[i])
        for i, (source, target) in enumerate(
            ((x_hbm, x_ref), (w_hbm, w), (b_hbm, b_ref), (u_hbm, u_ref)))
    ]
    for load in loads:
        load.start()
    barrier = pltpu.get_barrier_semaphore()
    for j in (1, 2, 3):
        ps, pd = partner(j)
        pl.semaphore_signal(barrier, inc=1, device_id=(g, c, ps, pd), device_id_type=MESH)
    for r in range(1, chans):
        pl.semaphore_signal(barrier, inc=1, device_id=(g, far(r)[0], s, d), device_id_type=MESH)

    def x_copy(index, j, plane):
        ps, pd = partner(j)
        return pltpu.make_async_remote_copy(
            src_ref=x_hbm.at[plane], dst_ref=xa.at[d, 2 * s + plane],
            send_sem=xa_send.at[index], recv_sem=xa_recv.at[index],
            device_id=(g, c, ps, pd), device_id_type=MESH)

    x_list = [(0, 2, o), (1, 2, s), (2, 1, 0), (3, 1, 1), (4, 3, 0), (5, 3, 1)]
    x_copies = [x_copy(*item) for item in x_list]

    def x_arrived(index, j, plane):
        ps, pd = partner(j)
        there = {0: s, 1: o}.get(index, plane)
        pltpu.make_async_remote_copy(
            src_ref=x_hbm.at[there], dst_ref=xa.at[pd, 2 * ps + there],
            send_sem=xa_send.at[index], recv_sem=xa_recv.at[index],
            device_id=(g, c, ps, pd), device_id_type=MESH).wait_recv()
        return pd, 2 * ps + there

    def blank_rows(ref, at):
        blank = jnp.zeros(ref.shape[-2:], ref.dtype)
        ref[at + (0,)] = blank
        ref[at + (width_y + 1,)] = blank

    for p in (0, 1):
        blank_rows(x3, (p,))

    def keep_columns(crop, plane, triple):
        xt[crop * gpq.shape[1] + plane] = triple.T

    loads[0].wait()
    triples = []
    for p in (0, 1):
        triple = z_shifted(x_ref[p])
        x3[p, pl.ds(1, width_y)] = triple.reshape(width_y, width_z, 3 * LANES)
        triples.append(triple)

    def taps_of(a, b):
        return pl.ds(9 * (a + 1) + 3 * (b + 1), 3)

    def rows_of(ref, b):
        return ref[pl.ds(1 + b, width_y)].reshape(area, -1)

    def partial_out(sources):
        left = jnp.concatenate([rows_of(ref, b) for ref, a in sources for b in (-1, 0, 1)], axis=1)
        right = jnp.concatenate(
            [w[taps_of(a, b)].reshape(3 * LANES, -1) for ref, a in sources for b in (-1, 0, 1)], axis=0)
        return jnp.dot(left, right, preferred_element_type=jnp.float32)

    def rs_copy(r, ph):
        return pltpu.make_async_remote_copy(
            src_ref=pb.at[ph, far(r)[0]], dst_ref=rb.at[ph, r - 1],
            send_sem=rs_send.at[r - 1, ph], recv_sem=rs_recv.at[r - 1, ph],
            device_id=(g, far(r)[0], s, d), device_id_type=MESH)

    def forward(ph, sources):
        total = partial_out(sources)
        for t in range(chans):
            part = total[:, t * LANES : (t + 1) * LANES]
            acc[ph, t] = part
            pb[ph, t] = part.astype(pb.dtype)

    def scatter(ph):
        for r in range(1, chans):
            rs_copy(r, ph).start()

    loads[1].wait()
    lean = 1 - 2 * s
    forward(0, [(x3.at[s], 0), (x3.at[o], lean)])
    pl.semaphore_wait(barrier, 3 + chans - 1)
    scatter(0)
    for copy in x_copies:
        copy.start()
    blank_rows(h3, ())
    for t in range(chans):
        for p in (0, 1):
            blank_rows(gpf, (t, p))
    planes = gpq.shape[1]
    for crop in range(gpq.shape[0]):
        for p in range(planes):
            blank_rows(gpq, (crop, p))
    at = x_arrived(*x_list[0])
    halo = z_shifted(xa[at])
    h3[pl.ds(1, width_y)] = halo.reshape(width_y, width_z, 3 * LANES)
    forward(1, [(x3.at[o], 0), (x3.at[s], -lean), (h3, lean)])
    scatter(1)
    keep_columns(*at, halo)
    for p in (0, 1):
        keep_columns(d, 2 * s + p, triples[p])
    for item in x_list[1:]:
        at = x_arrived(*item)
        keep_columns(*at, z_shifted(xa[at]))

    def ag_copy(r, ph):
        block = gpf.at[c, order[ph], pl.ds(1, width_y)]
        return pltpu.make_async_remote_copy(
            src_ref=block, dst_ref=block,
            send_sem=ag_send.at[r - 1, ph], recv_sem=ag_recv.at[r - 1, ph],
            device_id=(g, far(r)[0], s, d), device_id_type=MESH)

    def ag_arrived(r, ph):
        block = gpf.at[far(r)[1], order[ph], pl.ds(1, width_y)]
        pltpu.make_async_remote_copy(
            src_ref=block, dst_ref=block,
            send_sem=ag_send.at[r - 1, ph], recv_sem=ag_recv.at[r - 1, ph],
            device_id=(g, far(r)[0], s, d), device_id_type=MESH).wait_recv()

    loads[2].wait()
    loads[3].wait()
    for ph in (0, 1):
        plane = order[ph]
        preact = acc[ph, c] + b_ref[...]
        for r in range(1, chans):
            rs_copy(r, ph).wait_recv()
            preact = preact + rb[ph, r - 1].astype(jnp.float32)
        gate = jax.nn.sigmoid(preact)
        act_ref[plane] = (preact * gate).astype(act_ref.dtype).reshape(width_y, width_z, LANES)
        up = u_ref[plane].reshape(area, LANES).astype(jnp.float32)
        grad = up * gate * (1.0 + preact * (1.0 - gate))
        gpf[c, plane, pl.ds(1, width_y)] = grad.astype(gpf.dtype).reshape(width_y, width_z, LANES)
        for r in range(1, chans):
            ag_copy(r, ph).start()

    def gq_copy(t, j, ph, crop, where):
        return pltpu.make_async_remote_copy(
            src_ref=gpf.at[t, order[ph], pl.ds(1, width_y)],
            dst_ref=gpq.at[crop, where, pl.ds(1, width_y)],
            send_sem=gq_send.at[j - 1, ph], recv_sem=gq_recv.at[j - 1, ph],
            device_id=(g, c, t // 2, t % 2), device_id_type=MESH)

    def spread(ph):
        here = 2 * s + order[ph]
        for r in range(chans):
            t = far(r)[1]
            if r:
                ag_arrived(r, ph)
            j = 2 * lax.rem(t // 2 + s, 2) + lax.rem(t % 2 + d, 2)

            @pl.when(t != mine)
            def _(t=t, j=j):
                gq_copy(t, j, ph, d, here).start()

            @pl.when(t == mine)
            def _(t=t):
                gpq[d, here, pl.ds(1, width_y)] = gpf[t, order[ph], pl.ds(1, width_y)]

    def back(plane, a):
        left = jnp.concatenate(
            [gpf[t, plane, pl.ds(1 - b, width_y)].reshape(area, LANES)
             for b in (-1, 0, 1) for t in range(chans)], axis=1)
        right = jnp.concatenate(
            [w[taps_of(a, b)].reshape(3 * LANES, -1) for b in (-1, 0, 1)], axis=1)
        triple = lax.dot_general(
            left, right, (((1,), (1,)), ((), ())), preferred_element_type=jnp.float32)
        return z_combined(triple, width_z)

    def collected(ph):
        for j in (1, 2, 3):
            ps, pd = partner(j)
            there = ps if ph == 0 else 1 - ps
            gq_copy(2 * ps + pd, j, ph, pd, 2 * ps + there).wait_recv()

    def weight_part(ph):
        held = (0, 3) if ph == 0 else (1, 2)
        crops = range(gpq.shape[0])

        def step(i, carry):
            for a in (-1, 0, 1):
                pairs = [(crop, v) for crop in crops for v in held if 0 <= v + a < planes]
                left = jnp.concatenate([xt[crop * planes + v + a] for crop, v in pairs], axis=1)
                right = jnp.concatenate(
                    [gpq[crop, v, pl.ds(2 - i, width_y)].reshape(area, LANES) for crop, v in pairs],
                    axis=0)
                product = jnp.dot(left, right, preferred_element_type=jnp.float32)
                product = product.reshape(3, LANES, LANES)
                at = pl.ds(9 * (a + 1) + 3 * i, 3)
                gw_ref[at] = product if ph == 0 else gw_ref[at] + product
            return carry

        lax.fori_loop(0, 3, step, 0)

    spread(0)
    gi32[0] = back(s, 0)
    gi32[1] = back(s, lean)
    collected(0)
    weight_part(0)
    spread(1)
    hs[...] = back(o, lean).astype(hs.dtype)
    edge = pltpu.make_async_remote_copy(
        src_ref=hs, dst_ref=hr, send_sem=hb_send, recv_sem=hb_recv,
        device_id=(g, c, o, d), device_id_type=MESH)
    edge.start()
    gi_ref[s] = (gi32[0] + back(o, -lean)).astype(gi_ref.dtype).reshape(width_y, width_z, LANES)
    gi32[1] = gi32[1] + back(o, 0)
    collected(1)
    weight_part(1)

    edge.wait_recv()
    gi_ref[o] = (gi32[1] + hr[...].astype(jnp.float32)).astype(gi_ref.dtype).reshape(
        width_y, width_z, LANES)

    edge.wait_send()
    for copy in x_copies:
        copy.wait_send()
    for ph in (0, 1):
        for r in range(1, chans):
            rs_copy(r, ph).wait_send()
            ag_copy(r, ph).wait_send()
        for j in (1, 2, 3):
            ps, pd = partner(j)
            gq_copy(2 * ps + pd, j, ph, d, 2 * s + order[ph]).wait_send()


def local_fused(inputs, weights, bias, upstream):
    _, width_x, width_y, width_z, lanes = inputs.shape
    tap_count, _, outputs_all = weights.shape
    chans, crops = lax.axis_size("chan"), lax.axis_size("dp")
    planes = width_x * lax.axis_size("space")
    area = width_y * width_z
    half, full = jnp.bfloat16, jnp.float32
    slab = (width_x, width_y, width_z, lanes)
    dma = pltpu.SemaphoreType.DMA
    vmem = pl.BlockSpec(memory_space=pltpu.VMEM)
    flops = 3 * 2 * width_x * area * tap_count * lanes * outputs_all
    activated, grad_inputs, grad_weights = pl.pallas_call(
        functools.partial(fused_kernel, chans),
        out_shape=[
            jax.ShapeDtypeStruct(slab, full),
            jax.ShapeDtypeStruct(slab, full),
            jax.ShapeDtypeStruct((tap_count, lanes, lanes), full),
        ],
        in_specs=[pl.BlockSpec(memory_space=pltpu.HBM)] * 4,
        out_specs=[vmem] * 3,
        scratch_shapes=[
            pltpu.VMEM(slab, half),
            pltpu.VMEM((1, lanes), full),
            pltpu.VMEM(slab, half),
            pltpu.VMEM(weights.shape, half),
            pltpu.VMEM((crops, planes, width_y, width_z, lanes), half),
            pltpu.VMEM((width_x, width_y + 2, width_z, 3 * lanes), half),
            pltpu.VMEM((width_y + 2, width_z, 3 * lanes), half),
            pltpu.VMEM((crops * planes, 3 * lanes, area), half),
            pltpu.VMEM((2, chans, area, lanes), full),
            pltpu.VMEM((2, chans, area, lanes), half),
            pltpu.VMEM((2, chans - 1, area, lanes), half),
            pltpu.VMEM((chans, width_x, width_y + 2, width_z, lanes), half),
            pltpu.VMEM((crops, planes, width_y + 2, width_z, lanes), half),
            pltpu.VMEM((2, area, lanes), full),
            pltpu.VMEM((area, lanes), half),
            pltpu.VMEM((area, lanes), half),
            dma((4,)), dma((6,)), dma((6,)),
            dma((chans - 1, 2)), dma((chans - 1, 2)),
            dma((chans - 1, 2)), dma((chans - 1, 2)),
            dma((3, 2)), dma((3, 2)), dma, dma,
        ],
        compiler_params=pltpu.CompilerParams(
            collective_id=0, has_side_effects=True, vmem_limit_bytes=60 * 1024 * 1024),
        cost_estimate=pl.CostEstimate(
            flops=flops, bytes_accessed=2 * weights.size + 4 * tap_count * lanes * lanes,
            transcendentals=width_x * area * lanes),
    )(inputs.reshape(slab), weights, bias.reshape(1, lanes), upstream.reshape(slab))
    scale = 1.0 / math.sqrt(crops * planes * area)
    return activated[None].astype(half), grad_inputs[None].astype(half), grad_weights * scale


def local(inputs, weights, bias, upstream):
    fits = (
        inputs.shape[0] == 1
        and inputs.shape[1] == 2
        and inputs.shape[3] % 16 == 0
        and inputs.shape[4] == upstream.shape[4] == LANES
        and weights.shape[2] == LANES * lax.axis_size("chan")
        and lax.axis_size("chan") == 4
        and lax.axis_size("space") == 2
        and lax.axis_size("dp") == 2
    )
    return (local_fused if fits else local_plain)(inputs, weights, bias, upstream)


def solution(mesh):
    return jax.shard_map(
        local,
        mesh=mesh,
        in_specs=(
            P(("groups", "dp"), "space", None, None, "chan"),
            P(None, "chan", None),
            P("chan"),
            P(("groups", "dp"), "space", None, None, "chan"),
        ),
        out_specs=(
            P(("groups", "dp"), "space", None, None, "chan"),
            P(("groups", "dp"), "space", None, None, "chan"),
            P("groups", "chan", ("space", "dp")),
        ),
        check_vma=False,
    )
```
